32 devices in a mesh: fsdp: 16 (over z, y, core), tp: 2 (over x).
Axes of the slice: x: 2, y: 2, z: 4, core: 2. Of those that a mesh axis runs over, the one named last changes fastest.
Arguments:
- tokens: bfloat16 [512, 8192], P('tp', 'fsdp'), may hold values from -6 to 6
- gate_blocks: bfloat16 [256, 22, 128, 128], P(('fsdp', 'tp')), may hold values from -0.109375 to 0.109375
- up_blocks: bfloat16 [256, 22, 128, 128], P(('fsdp', 'tp')), may hold values from -0.109375 to 0.109375
- down_blocks: bfloat16 [256, 22, 128, 128], P(('fsdp', 'tp')), may hold values from -0.0546875 to 0.0546875
- gate_index: int32 [256, 22], P('fsdp'), may hold values from 0 to 63, as said below
- up_index: int32 [256, 22], P('fsdp'), may hold values from 0 to 63, as said below
- down_index: int32 [256, 22], P('fsdp'), may hold values from 0 to 63, as said below
- gate_count: int32 [256], P('fsdp'), may hold values from 14 to 22
- up_count: int32 [256], P('fsdp'), may hold values from 14 to 22
- down_count: int32 [256], P('fsdp'), may hold values from 14 to 22
Outputs:
- mixed: bfloat16 [512, 8192], P('tp', 'fsdp')
The draws below stay inside these ranges and needn't reach their ends.
Inputs may be any that keep to these rules, and one draw needn't show every extreme that they name: `gate_index`: in each row the first gate_count entries name the kept row blocks of that block column; the 22 entries of a row are different numbers. `up_index`: in each row the first up_count entries name the kept row blocks of that block column; the 22 entries of a row are different numbers. `down_index`: in each row the first down_count entries name the kept column blocks of that block row; the 22 entries of a row are different numbers.
All inputs are finite; a program needn't handle non-finite values.
Results may differ from the reference program's by a relative error of at most 0.0049.
Values may be sent and summed in bfloat16 or wider, within the bound.
A program may use at most 256 MiB of HBM per device.

```python
import jax
import jax.numpy as jnp
from jax import lax

D = 8192
F = 32768
BLK = 128
KMAX = 22
KMIN = 14
TOKENS = 512
DB = 64
FB = 256


def draw_index_rows(key):
    row_keys = jax.random.split(key, FB)
    orders = jax.vmap(lambda one_key: jax.random.permutation(one_key, DB))(row_keys)
    return orders[:, :KMAX].astype(jnp.int32)


def draw_count_rows(key):
    first_key, second_key, third_key = jax.random.split(key, 3)
    counts = jax.random.randint(first_key, (FB,), KMIN, KMAX + 1).astype(jnp.int32)
    top_pos = jax.random.randint(second_key, (), 0, FB)
    low_pos = (top_pos + 1 + jax.random.randint(third_key, (), 0, FB - 1)) % FB
    counts = counts.at[top_pos].set(KMAX)
    counts = counts.at[low_pos].set(KMIN)
    return counts


def draw_gate_index(key, part):
    return draw_index_rows(jax.random.fold_in(key, 101))


def draw_up_index(key, part):
    return draw_index_rows(jax.random.fold_in(key, 202))


def draw_down_index(key, part):
    return draw_index_rows(jax.random.fold_in(key, 303))


def draw_gate_count(key, part):
    return draw_count_rows(jax.random.fold_in(key, 404))


def draw_up_count(key, part):
    return draw_count_rows(jax.random.fold_in(key, 505))


def draw_down_count(key, part):
    return draw_count_rows(jax.random.fold_in(key, 606))


def block_levels(stream_key, dims, pieces, least, high):
    factor_of, own = 1.0, jax.random.fold_in(stream_key, 6)
    for dim, parts in pieces:
        draws = jnp.exp(jax.random.uniform(jax.random.fold_in(own, dim), (parts,), jnp.float32, least / len(pieces), high / len(pieces)))
        factor_of = factor_of * jnp.repeat(draws, dims[dim] // parts).reshape([-1 if axis == dim else 1 for axis in range(len(dims))])
    return factor_of


def centred(key, shape, deviation, bound, pieces=(), held_as=jnp.bfloat16):
    level = block_levels(key, shape, pieces, -0.22, 0.18) if pieces else 1.0
    array = jax.random.normal(key, shape, jnp.float32) * deviation * level
    return jnp.minimum(jnp.maximum(array, -bound), bound).astype(held_as)


def setup_inputs(seed: int = 0) -> dict:
    seeds = jax.random.split(jax.random.key(seed), 11)
    return {
        "tokens": centred(seeds[0], (TOKENS, D), 1.0, 6.0, ((0, 2), (1, 16))),
        "gate_blocks": centred(seeds[1], (FB, KMAX, BLK, BLK), (KMAX * BLK) ** -0.5, 0.109375, ((0, 32),)),
        "up_blocks": centred(seeds[2], (FB, KMAX, BLK, BLK), (KMAX * BLK) ** -0.5, 0.109375, ((0, 32),)),
        "down_blocks": centred(seeds[3], (FB, KMAX, BLK, BLK), (F * KMAX // DB) ** -0.5, 0.0546875, ((0, 32),)),
        "gate_index": draw_gate_index(jax.random.fold_in(seeds[10], 71), 0),
        "up_index": draw_up_index(jax.random.fold_in(seeds[10], 71), 0),
        "down_index": draw_down_index(jax.random.fold_in(seeds[10], 71), 0),
        "gate_count": draw_gate_count(jax.random.fold_in(seeds[10], 71), 0),
        "up_count": draw_up_count(jax.random.fold_in(seeds[10], 71), 0),
        "down_count": draw_down_count(jax.random.fold_in(seeds[10], 71), 0),
    }


def project_in(tile_grid, block_set, row_ids, kept_num):
    token_rows = tile_grid.shape[0]
    slot_num = row_ids.shape[1]
    side_len = tile_grid.shape[2]

    def column_block(packed):
        blocks_one, ids_one, count_one = packed
        live_mask = (jnp.arange(slot_num) < count_one).astype(blocks_one.dtype)
        selected = tile_grid[:, ids_one, :].reshape(token_rows, slot_num * side_len)
        panel_mat = (blocks_one * live_mask[:, None, None]).reshape(slot_num * side_len, side_len)
        return jnp.dot(selected, panel_mat, preferred_element_type=jnp.float32)

    column_out = lax.map(column_block, (block_set, row_ids, kept_num))
    return jnp.transpose(column_out, (1, 0, 2)).reshape(token_rows, -1)


def project_out(hidden, block_set, col_ids, kept_num, row_blocks):
    token_rows = hidden.shape[0]
    slot_num = col_ids.shape[1]
    side_len = block_set.shape[2]
    hid_tiles = jnp.transpose(hidden.reshape(token_rows, -1, side_len), (1, 0, 2))

    def advance(running, packed):
        blocks_one, ids_one, count_one, hid_tile = packed
        live_mask = (jnp.arange(slot_num) < count_one).astype(blocks_one.dtype)
        panel_mat = jnp.transpose(blocks_one * live_mask[:, None, None], (1, 0, 2)).reshape(side_len, slot_num * side_len)
        product = jnp.dot(hid_tile, panel_mat, preferred_element_type=jnp.float32).reshape(token_rows, slot_num, side_len)
        return running.at[:, ids_one, :].add(product), None

    start_sum = jnp.zeros((token_rows, row_blocks, side_len), jnp.float32)
    running, _ = lax.scan(advance, start_sum, (block_set, col_ids, kept_num, hid_tiles))
    return running.reshape(token_rows, row_blocks * side_len)


def reference(tokens, gate_blocks, up_blocks, down_blocks, gate_index, up_index, down_index, gate_count, up_count, down_count):
    token_rows = tokens.shape[0]
    side_len = gate_blocks.shape[2]
    row_blocks = tokens.shape[1] // side_len
    tile_grid = tokens.reshape(token_rows, row_blocks, side_len)
    gate = project_in(tile_grid, gate_blocks, gate_index, gate_count)
    up_val = project_in(tile_grid, up_blocks, up_index, up_count)
    hidden = (jax.nn.silu(gate) * up_val).astype(jnp.bfloat16)
    mixed = project_out(hidden, down_blocks, down_index, down_count, row_blocks)
    return mixed.astype(jnp.bfloat16)
```

```python
import functools

import jax
import jax.numpy as jnp
from jax import lax
from jax.experimental import pallas as pl
from jax.experimental.pallas import tpu as pltpu
from jax.sharding import PartitionSpec as P

MESH = pl.DeviceIdType.MESH
VMEM_BYTES = 56 * 1024 * 1024


def kept_mask(count_part, slot_num):
    return jnp.arange(slot_num, dtype=jnp.int32)[None, :] < count_part[:, None]


def general_body(
    tokens,
    gate_blocks,
    up_blocks,
    down_blocks,
    gate_index,
    up_index,
    down_index,
    gate_count,
    up_count,
    down_count,
):
    whole = lax.all_gather(tokens, "fsdp", axis=1, tiled=True)
    side_len = gate_blocks.shape[-1]
    row_blocks = whole.shape[1] // side_len
    slot_num = gate_index.shape[1]
    block_ids = jnp.arange(row_blocks, dtype=jnp.int32)

    def onehot_of(index_part, count_part):
        live_mask = kept_mask(count_part, slot_num)
        return (
            (index_part[:, :, None] == block_ids[None, None, :]) & live_mask[:, :, None]
        ).astype(jnp.bfloat16)

    def project_in(block_set, index_part, count_part):
        onehot = onehot_of(index_part, count_part)
        panel = jnp.einsum("jki,jkcd->icjd", onehot, block_set, preferred_element_type=jnp.bfloat16)
        panel = panel.reshape(row_blocks * side_len, index_part.shape[0] * side_len)
        return jnp.dot(whole, panel, preferred_element_type=jnp.float32)

    gate_part = project_in(
        lax.all_gather(gate_blocks, "tp", axis=0, tiled=True), gate_index, gate_count
    )
    up_part = project_in(lax.all_gather(up_blocks, "tp", axis=0, tiled=True), up_index, up_count)
    hidden = (jax.nn.silu(gate_part) * up_part).astype(jnp.bfloat16)
    piece = lax.all_gather(down_blocks, "tp", axis=0, tiled=True)
    panel = jnp.einsum(
        "jki,jkcd->jcid",
        onehot_of(down_index, down_count),
        piece,
        preferred_element_type=jnp.bfloat16,
    )
    panel = panel.reshape(piece.shape[0] * side_len, row_blocks * side_len)
    partial_out = jnp.dot(hidden, panel, preferred_element_type=jnp.float32)
    return lax.psum_scatter(partial_out, "fsdp", scatter_dimension=1, tiled=True).astype(
        jnp.bfloat16
    )


class Place:
    def __init__(self, depth):
        fs = lax.axis_index("fsdp")
        self.depth = depth
        self.fs = fs
        self.x = lax.axis_index("tp")
        self.c = fs % 2
        self.y = (fs // 2) % 2
        self.z = fs // 4

    def spot(self, s, z, c):
        across_a, across_b = s % 2, s // 2
        dx = across_b * (1 - c) + across_a * c
        dy = across_a * (1 - c) + across_b * c
        return (z * 2 + (self.y + dy) % 2) * 2 + c, (self.x + dx) % 2

    def behind(self, d):
        return (self.z + self.depth - d) % self.depth

    def ahead(self, d):
        return (self.z + d) % self.depth

    def device(self, s):
        f, t = self.spot(s, self.z, self.c)
        return {"fsdp": f, "tp": t}

    def other_core(self):
        return {"fsdp": self.fs + 1 - 2 * self.c, "tp": self.x}

    def along_z(self, d):
        return {"fsdp": (self.ahead(d) * 2 + self.y) * 2 + self.c, "tp": self.x}


def greet(place):
    barrier = pltpu.get_barrier_semaphore()
    partners = [place.device(1), place.device(2), place.other_core()]
    partners += [place.along_z(d) for d in range(1, place.depth)]
    for partner in partners:
        pl.semaphore_signal(barrier, inc=1, device_id=partner, device_id_type=MESH)
    pl.semaphore_wait(barrier, len(partners))


def remote(src, dst, send_sem, recv_sem, device):
    return pltpu.make_async_remote_copy(
        src_ref=src,
        dst_ref=dst,
        send_sem=send_sem,
        recv_sem=recv_sem,
        device_id=device,
        device_id_type=MESH,
    )


def in_kernel(
    depth,
    slot_of,
    tokens,
    gate_hbm,
    up_hbm,
    hidden,
    tok,
    weights,
    acc,
    load_sem,
    z_send,
    a_send,
    b_send,
    c_send,
    plane_recv,
    core_recv,
):
    place = Place(depth)
    cols, slots = gate_hbm.shape[0], gate_hbm.shape[1]
    side = gate_hbm.shape[2]
    rows = tokens.shape[0]
    group = tokens.shape[1] // side
    pairs = cols // 2

    loads = [
        pltpu.make_async_copy(src, weights.at[m, :, pl.ds(0, slots)], load_sem.at[m])
        for m, src in enumerate((gate_hbm, up_hbm))
    ]
    for load in loads:
        load.start()
    tok[place.fs, place.x] = tokens[...]
    greet(place)

    def shard(s, d):
        f, t = place.spot(s, place.behind(d), place.c)
        return tok.at[f, t]

    def to_a(d):
        return remote(shard(0, d), shard(0, d), a_send.at[d], plane_recv.at[1, d], place.device(1))

    def to_b(s, d):
        return remote(
            shard(s, d), shard(s, d), b_send.at[s, d], plane_recv.at[s + 2, d], place.device(2)
        )

    def to_core(s, d):
        return remote(
            shard(s, d), shard(s, d), c_send.at[s, d], core_recv.at[s, d], place.other_core()
        )

    def to_z(d):
        return remote(
            shard(0, 0), shard(0, 0), z_send.at[d], plane_recv.at[0, d], place.along_z(d)
        )

    def arrived(s, d):
        ref = shard(s, d)
        remote(ref, ref, c_send.at[s, d], plane_recv.at[s, d], place.other_core()).wait_recv()

    def arrived_core(s, d):
        f, t = place.spot(s, place.behind(d), 1 - place.c)
        ref = tok.at[f, t]
        remote(ref, ref, c_send.at[s, d], core_recv.at[s, d], place.other_core()).wait_recv()

    to_a(0).start()
    to_b(0, 0).start()
    for d in range(1, depth):
        to_z(d).start()
    to_core(0, 0).start()

    weights[:, :, slots] = jnp.zeros((2, cols, side, side), weights.dtype)
    acc[...] = jnp.zeros_like(acc)
    for load in loads:
        load.wait()

    def multiply(d, dy, c):
        f = (place.behind(d) * 2 + (place.y + dy) % 2) * 2 + c
        left = tok[f].reshape(2 * rows, group * side)

        def pair(n, carry):
            for m in range(2):
                panel = jnp.concatenate(
                    [
                        jnp.concatenate(
                            [
                                weights[m, 2 * n + e, slot_of[m * cols + 2 * n + e, f * group + i]]
                                for e in range(2)
                            ],
                            axis=1,
                        )
                        for i in range(group)
                    ],
                    axis=0,
                )
                acc[m, n] += jnp.dot(left, panel, preferred_element_type=jnp.float32)
            return carry

        lax.fori_loop(0, pairs, pair, 0)

    def stage(d, carry):
        @pl.when(d + 1 < depth)
        def _():
            arrived(0, d + 1)
            to_a(d + 1).start()
            to_b(0, d + 1).start()
            to_core(0, d + 1).start()

        arrived(1, d)
        to_b(1, d).start()
        to_core(1, d).start()
        arrived(2, d)
        to_core(2, d).start()
        multiply(d, 0, place.c)
        arrived(3, d)
        to_core(3, d).start()
        for s in range(3):
            arrived_core(s, d)
        multiply(d, 0, 1 - place.c)
        multiply(d, 1, place.c)
        arrived_core(3, d)
        multiply(d, 1, 1 - place.c)
        return carry

    lax.fori_loop(0, depth, stage, 0)

    for n in range(pairs):
        gate = acc[0, n]
        up = acc[1, n]
        out = (gate / (1.0 + jnp.exp(-gate)) * up).astype(hidden.dtype)
        hidden[:, :, n * 2 * side : (n + 1) * 2 * side] = out.reshape(2, rows, 2 * side)

    for d in range(depth):
        if d:
            to_z(d).wait_send()
        to_a(d).wait_send()
        for s in range(2):
            to_b(s, d).wait_send()
        for s in range(4):
            to_core(s, d).wait_send()


def out_kernel(
    depth,
    slot_of,
    hidden,
    down_hbm,
    mixed,
    weights,
    total,
    core_out,
    core_in,
    b_out,
    b_in,
    a_out,
    a_in,
    z_out,
    z_in,
    load_sem,
    c_send,
    c_recv,
    b_send,
    b_recv,
    a_send,
    a_recv,
    z_send,
    z_recv,
):
    place = Place(depth)
    cols, slots, side = down_hbm.shape[0], down_hbm.shape[1], down_hbm.shape[2]
    group = mixed.shape[1] // side
    pairs = group // 2

    load = pltpu.make_async_copy(down_hbm, weights.at[:, pl.ds(0, slots)], load_sem)
    load.start()
    weights[:, slots] = jnp.zeros((cols, side, side), weights.dtype)
    greet(place)
    load.wait()

    def share(f, t, store):
        left = hidden[t]
        for n in range(pairs):
            panel = jnp.concatenate(
                [
                    jnp.concatenate(
                        [weights[j, slot_of[j, f * group + 2 * n + e]] for e in range(2)], axis=1
                    )
                    for j in range(cols)
                ],
                axis=0,
            )
            store(
                slice(n * 2 * side, (n + 1) * 2 * side),
                jnp.dot(left, panel, preferred_element_type=jnp.float32),
            )

    def to_core(s, d):
        return remote(
            core_out.at[s, d],
            core_in.at[s, d],
            c_send.at[s, d],
            c_recv.at[s, d],
            place.other_core(),
        )

    def to_b(s, d):
        return remote(
            b_out.at[s, d], b_in.at[s, d], b_send.at[s, d], b_recv.at[s, d], place.device(2)
        )

    def to_a(d):
        return remote(a_out.at[d], a_in.at[d], a_send.at[d], a_recv.at[d], place.device(1))

    def to_z(d):
        return remote(z_out.at[d], z_in.at[d], z_send.at[d], z_recv.at[d], place.along_z(d))

    for s in (3, 2, 1, 0):

        def step(k, carry, s=s):
            d = (k + 1) % depth
            f, t = place.spot(s, place.ahead(d), 1 - place.c)

            def store_out(where, value):
                core_out[s, d, :, where] = value.astype(core_out.dtype)

            share(f, t, store_out)
            to_core(s, d).start()
            f, t = place.spot(s, place.ahead(d), place.c)

            def store_own(where, value):
                total[s, d, :, where] = value

            share(f, t, store_own)
            to_core(s, d).wait_recv()
            value = total[s, d] + core_in[s, d].astype(jnp.float32)
            if s >= 2:
                b_out[s - 2, d] = value.astype(b_out.dtype)
                to_b(s - 2, d).start()
            else:
                total[s, d] = value
            return carry

        lax.fori_loop(0, depth, step, 0)

    def cross_a(k, carry):
        d = (k + 1) % depth
        to_b(1, d).wait_recv()
        a_out[d] = (total[1, d] + b_in[1, d].astype(jnp.float32)).astype(a_out.dtype)
        to_a(d).start()
        return carry

    lax.fori_loop(0, depth, cross_a, 0)

    def cross_z(k, carry):
        d = (k + 1) % depth
        to_b(0, d).wait_recv()
        to_a(d).wait_recv()
        value = total[0, d] + b_in[0, d].astype(jnp.float32) + a_in[d].astype(jnp.float32)

        @pl.when(d > 0)
        def _():
            z_out[d] = value.astype(z_out.dtype)
            to_z(d).start()

        @pl.when(d == 0)
        def _():
            total[0, d] = value

        return carry

    lax.fori_loop(0, depth, cross_z, 0)
    value = total[0, 0]
    for d in range(1, depth):
        to_z(d).wait_recv()
        value = value + z_in[d].astype(jnp.float32)
    mixed[...] = value.astype(mixed.dtype)

    for d in range(depth):
        if d:
            to_z(d).wait_send()
        to_a(d).wait_send()
        for s in range(2):
            to_b(s, d).wait_send()
        for s in range(4):
            to_core(s, d).wait_send()


def plane_body(
    depth,
    tokens,
    gate_blocks,
    up_blocks,
    down_blocks,
    gate_index,
    up_index,
    down_index,
    gate_count,
    up_count,
    down_count,
):
    rows, feats = tokens.shape
    cols, slots, side = gate_blocks.shape[:3]
    fsdp = 4 * depth
    row_blocks = fsdp * feats // side
    bf16 = tokens.dtype

    first = lax.axis_index("tp") * cols
    index = jnp.stack([gate_index, up_index, down_index])
    count = jnp.stack([gate_count, up_count, down_count])
    index = lax.dynamic_slice_in_dim(index, first, cols, 1)
    count = lax.dynamic_slice_in_dim(count, first, cols, 1)
    slot_ids = jnp.arange(slots, dtype=jnp.int32)[None, None, :, None]
    block_ids = jnp.arange(row_blocks, dtype=jnp.int32)[None, None, None, :]
    hit = (index[..., None] == block_ids) & (slot_ids < count[:, :, None, None])
    slot_of = jnp.min(jnp.where(hit, slot_ids, slots), axis=2)

    vmem = pl.BlockSpec(memory_space=pltpu.VMEM)
    smem = pl.BlockSpec(memory_space=pltpu.SMEM)
    anywhere = pl.BlockSpec(memory_space=pl.ANY)
    dma = pltpu.SemaphoreType.DMA

    hidden = pl.pallas_call(
        functools.partial(in_kernel, depth),
        out_shape=jax.ShapeDtypeStruct((2, rows, cols * side), bf16),
        in_specs=[smem, vmem, anywhere, anywhere],
        out_specs=vmem,
        scratch_shapes=[
            pltpu.VMEM((fsdp, 2, rows, feats), bf16),
            pltpu.VMEM((2, cols, slots + 1, side, side), bf16),
            pltpu.VMEM((2, cols // 2, 2 * rows, 2 * side), jnp.float32),
            dma((2,)),
            dma((depth,)),
            dma((depth,)),
            dma((2, depth)),
            dma((4, depth)),
            dma((4, depth)),
            dma((4, depth)),
        ],
        compiler_params=pltpu.CompilerParams(
            collective_id=0, has_side_effects=True, vmem_limit_bytes=VMEM_BYTES
        ),
    )(slot_of[:2].reshape(2 * cols, row_blocks), tokens, gate_blocks, up_blocks)

    return pl.pallas_call(
        functools.partial(out_kernel, depth),
        out_shape=jax.ShapeDtypeStruct((rows, feats), bf16),
        in_specs=[smem, vmem, anywhere],
        out_specs=vmem,
        scratch_shapes=[
            pltpu.VMEM((cols, slots + 1, side, side), bf16),
            pltpu.VMEM((4, depth, rows, feats), jnp.float32),
            pltpu.VMEM((4, depth, rows, feats), bf16),
            pltpu.VMEM((4, depth, rows, feats), bf16),
            pltpu.VMEM((2, depth, rows, feats), bf16),
            pltpu.VMEM((2, depth, rows, feats), bf16),
            pltpu.VMEM((depth, rows, feats), bf16),
            pltpu.VMEM((depth, rows, feats), bf16),
            pltpu.VMEM((depth, rows, feats), bf16),
            pltpu.VMEM((depth, rows, feats), bf16),
            dma(()),
            dma((4, depth)),
            dma((4, depth)),
            dma((2, depth)),
            dma((2, depth)),
            dma((depth,)),
            dma((depth,)),
            dma((depth,)),
            dma((depth,)),
        ],
        compiler_params=pltpu.CompilerParams(
            collective_id=1, has_side_effects=True, vmem_limit_bytes=VMEM_BYTES
        ),
    )(slot_of[2], hidden, down_blocks)


def solution(mesh):
    fsdp, tp = mesh.shape["fsdp"], mesh.shape["tp"]
    if tp == 2 and fsdp % 4 == 0:
        body = functools.partial(plane_body, fsdp // 4)
    else:
        body = general_body
    in_specs = (
        P("tp", "fsdp"),
        P(("fsdp", "tp"), None, None, None),
        P(("fsdp", "tp"), None, None, None),
        P(("fsdp", "tp"), None, None, None),
        P("fsdp", None),
        P("fsdp", None),
        P("fsdp", None),
        P("fsdp"),
        P("fsdp"),
        P("fsdp"),
    )
    out_specs = P("tp", "fsdp")
    return jax.shard_map(body, mesh=mesh, in_specs=in_specs, out_specs=out_specs, check_vma=False)
```

```python
import functools

import jax
import jax.numpy as jnp
from jax import lax
from jax.experimental import pallas as pl
from jax.experimental.pallas import tpu as pltpu
from jax.sharding import PartitionSpec as P

MESH = pl.DeviceIdType.MESH
VMEM_BYTES = 56 * 1024 * 1024


def kept_mask(count_part, slot_num):
    return jnp.arange(slot_num, dtype=jnp.int32)[None, :] < count_part[:, None]


def general_body(
    tokens,
    gate_blocks,
    up_blocks,
    down_blocks,
    gate_index,
    up_index,
    down_index,
    gate_count,
    up_count,
    down_count,
):
    whole = lax.all_gather(tokens, "fsdp", axis=1, tiled=True)
    side_len = gate_blocks.shape[-1]
    row_blocks = whole.shape[1] // side_len
    slot_num = gate_index.shape[1]
    block_ids = jnp.arange(row_blocks, dtype=jnp.int32)

    def onehot_of(index_part, count_part):
        live_mask = kept_mask(count_part, slot_num)
        return (
            (index_part[:, :, None] == block_ids[None, None, :]) & live_mask[:, :, None]
        ).astype(jnp.bfloat16)

    def project_in(block_set, index_part, count_part):
        onehot = onehot_of(index_part, count_part)
        panel = jnp.einsum("jki,jkcd->icjd", onehot, block_set, preferred_element_type=jnp.bfloat16)
        panel = panel.reshape(row_blocks * side_len, index_part.shape[0] * side_len)
        return jnp.dot(whole, panel, preferred_element_type=jnp.float32)

    gate_part = project_in(
        lax.all_gather(gate_blocks, "tp", axis=0, tiled=True), gate_index, gate_count
    )
    up_part = project_in(lax.all_gather(up_blocks, "tp", axis=0, tiled=True), up_index, up_count)
    hidden = (jax.nn.silu(gate_part) * up_part).astype(jnp.bfloat16)
    piece = lax.all_gather(down_blocks, "tp", axis=0, tiled=True)
    panel = jnp.einsum(
        "jki,jkcd->jcid",
        onehot_of(down_index, down_count),
        piece,
        preferred_element_type=jnp.bfloat16,
    )
    panel = panel.reshape(piece.shape[0] * side_len, row_blocks * side_len)
    partial_out = jnp.dot(hidden, panel, preferred_element_type=jnp.float32)
    return lax.psum_scatter(partial_out, "fsdp", scatter_dimension=1, tiled=True).astype(
        jnp.bfloat16
    )


class Place:
    def __init__(self, depth):
        fs = lax.axis_index("fsdp")
        self.depth = depth
        self.fs = fs
        self.x = lax.axis_index("tp")
        self.c = fs % 2
        self.y = (fs // 2) % 2
        self.z = fs // 4

    def spot(self, s, z, c):
        across_a, across_b = s % 2, s // 2
        dx = across_b * (1 - c) + across_a * c
        dy = across_a * (1 - c) + across_b * c
        return (z * 2 + (self.y + dy) % 2) * 2 + c, (self.x + dx) % 2

    def order(self, j):
        below, above = self.z, self.depth - 1 - self.z
        near = jnp.minimum(below, above)
        far = j - near
        one_side = jnp.where(below > above, self.z - far, self.z + far)
        both = jnp.where(j % 2 == 1, self.z - (j + 1) // 2, self.z + j // 2)
        return jnp.where(j > 2 * near, one_side, both)

    def ahead(self, d):
        return (self.z + d) % self.depth

    def device(self, s):
        f, t = self.spot(s, self.z, self.c)
        return {"fsdp": f, "tp": t}

    def other_core(self):
        return {"fsdp": self.fs + 1 - 2 * self.c, "tp": self.x}

    def at_z(self, z):
        return {"fsdp": (z * 2 + self.y) * 2 + self.c, "tp": self.x}

    def along_z(self, d):
        return self.at_z(self.ahead(d))


def greet(place):
    barrier = pltpu.get_barrier_semaphore()
    partners = [place.device(1), place.device(2), place.other_core()]
    partners += [place.along_z(d) for d in range(1, place.depth)]
    for partner in partners:
        pl.semaphore_signal(barrier, inc=1, device_id=partner, device_id_type=MESH)
    pl.semaphore_wait(barrier, len(partners))


def remote(src, dst, send_sem, recv_sem, device):
    return pltpu.make_async_remote_copy(
        src_ref=src,
        dst_ref=dst,
        send_sem=send_sem,
        recv_sem=recv_sem,
        device_id=device,
        device_id_type=MESH,
    )


def in_kernel(
    depth,
    slot_of,
    tokens,
    gate_hbm,
    up_hbm,
    hidden,
    tok,
    weights,
    acc,
    load_sem,
    z_send,
    a_send,
    b_send,
    c_send,
    plane_recv,
    core_recv,
):
    place = Place(depth)
    cols, slots = gate_hbm.shape[0], gate_hbm.shape[1]
    side = gate_hbm.shape[2]
    rows = tokens.shape[0]
    group = tokens.shape[1] // side
    pairs = cols // 2

    loads = [
        pltpu.make_async_copy(src, weights.at[m, :, pl.ds(0, slots)], load_sem.at[m])
        for m, src in enumerate((gate_hbm, up_hbm))
    ]
    for load in loads:
        load.start()
    tok[place.fs, place.x] = tokens[...]
    greet(place)

    def shard(s, z, c):
        f, t = place.spot(s, z, c)
        return tok.at[f, t]

    def to_a(z):
        ref = shard(0, z, place.c)
        return remote(ref, ref, a_send.at[z], plane_recv.at[1, z], place.device(1))

    def to_b(s, z):
        ref = shard(s, z, place.c)
        return remote(ref, ref, b_send.at[s, z], plane_recv.at[s + 2, z], place.device(2))

    def to_core(s, z):
        ref = shard(s, z, place.c)
        return remote(ref, ref, c_send.at[s, z], core_recv.at[s, z], place.other_core())

    def to_z(up, z):
        ref = shard(0, z, place.c)
        device = place.at_z(place.z + 2 * up - 1)
        return remote(ref, ref, z_send.at[up, z], plane_recv.at[0, z], device)

    def arrived(s, z):
        ref = shard(s, z, place.c)
        remote(ref, ref, c_send.at[s, z], plane_recv.at[s, z], place.other_core()).wait_recv()

    def arrived_core(s, z):
        ref = shard(s, z, 1 - place.c)
        remote(ref, ref, c_send.at[s, z], core_recv.at[s, z], place.other_core()).wait_recv()

    def each_relay(z, act):
        pl.when((z <= place.z) & (place.z < depth - 1))(lambda: act(to_z(1, z)))
        pl.when((z >= place.z) & (place.z > 0))(lambda: act(to_z(0, z)))

    def begin(z):
        each_relay(z, lambda copy: copy.start())
        to_a(z).start()
        to_b(0, z).start()
        to_core(0, z).start()

    def take(j):
        z = place.order(j)
        arrived(0, z)
        begin(z)

    begin(place.z)

    weights[:, :, slots] = jnp.zeros((2, cols, side, side), weights.dtype)
    acc[...] = jnp.zeros_like(acc)
    for load in loads:
        load.wait()

    def multiply(z, dy, c):
        f = (z * 2 + (place.y + dy) % 2) * 2 + c
        left = tok[f].reshape(2 * rows, group * side)

        def pair(n, carry):
            for m in range(2):
                panel = jnp.concatenate(
                    [
                        jnp.concatenate(
                            [
                                weights[m, 2 * n + e, slot_of[m * cols + 2 * n + e, f * group + i]]
                                for e in range(2)
                            ],
                            axis=1,
                        )
                        for i in range(group)
                    ],
                    axis=0,
                )
                acc[m, n] += jnp.dot(left, panel, preferred_element_type=jnp.float32)
            return carry

        lax.fori_loop(0, pairs, pair, 0)

    def stage(j, carry):
        last = place.order(j - 1)

        @pl.when(j + 1 < depth)
        def _():
            take(j + 1)

        @pl.when(j < depth)
        def _():
            z = place.order(j)
            arrived(1, z)
            to_b(1, z).start()
            to_core(1, z).start()

        @pl.when(j > 0)
        def _():
            multiply(last, 0, place.c)

        @pl.when(j < depth)
        def _():
            z = place.order(j)
            arrived(2, z)
            to_core(2, z).start()

        @pl.when(j > 0)
        def _():
            multiply(last, 1, place.c)

        @pl.when(j < depth)
        def _():
            z = place.order(j)
            arrived(3, z)
            to_core(3, z).start()

        @pl.when(j > 0)
        def _():
            for s in range(4):
                arrived_core(s, last)
            multiply(last, 0, 1 - place.c)
            multiply(last, 1, 1 - place.c)

        return carry

    lax.fori_loop(0, depth + 1, stage, 0)

    for n in range(pairs):
        gate = acc[0, n]
        up = acc[1, n]
        out = (gate / (1.0 + jnp.exp(-gate)) * up).astype(hidden.dtype)
        hidden[:, :, n * 2 * side : (n + 1) * 2 * side] = out.reshape(2, rows, 2 * side)

    for z in range(depth):
        each_relay(z, lambda copy: copy.wait_send())
        to_a(z).wait_send()
        for s in range(2):
            to_b(s, z).wait_send()
        for s in range(4):
            to_core(s, z).wait_send()


def out_kernel(
    depth,
    slot_of,
    hidden,
    down_hbm,
    mixed,
    weights,
    total,
    core_out,
    core_in,
    b_out,
    b_in,
    a_out,
    a_in,
    z_out,
    z_in,
    load_sem,
    c_send,
    c_recv,
    b_send,
    b_recv,
    a_send,
    a_recv,
    z_send,
    z_recv,
):
    place = Place(depth)
    cols, slots, side = down_hbm.shape[0], down_hbm.shape[1], down_hbm.shape[2]
    group = mixed.shape[1] // side
    pairs = group // 2

    load = pltpu.make_async_copy(down_hbm, weights.at[:, pl.ds(0, slots)], load_sem)
    load.start()
    weights[:, slots] = jnp.zeros((cols, side, side), weights.dtype)
    greet(place)
    load.wait()

    def share(f, t, store):
        left = hidden[t]
        for n in range(pairs):
            panel = jnp.concatenate(
                [
                    jnp.concatenate(
                        [weights[j, slot_of[j, f * group + 2 * n + e]] for e in range(2)], axis=1
                    )
                    for j in range(cols)
                ],
                axis=0,
            )
            store(
                slice(n * 2 * side, (n + 1) * 2 * side),
                jnp.dot(left, panel, preferred_element_type=jnp.float32),
            )

    def to_core(s, d):
        return remote(
            core_out.at[s, d],
            core_in.at[s, d],
            c_send.at[s, d],
            c_recv.at[s, d],
            place.other_core(),
        )

    def to_b(s, d):
        return remote(
            b_out.at[s, d], b_in.at[s, d], b_send.at[s, d], b_recv.at[s, d], place.device(2)
        )

    def to_a(d):
        return remote(a_out.at[d], a_in.at[d], a_send.at[d], a_recv.at[d], place.device(1))

    def to_z(d):
        return remote(z_out.at[d], z_in.at[d], z_send.at[d], z_recv.at[d], place.along_z(d))

    def slab(k):
        return (k + 1) % depth

    def unit(s, d):
        f, t = place.spot(s, place.ahead(d), 1 - place.c)

        def store_out(where, value):
            core_out[s, d, :, where] = value.astype(core_out.dtype)

        share(f, t, store_out)
        to_core(s, d).start()
        f, t = place.spot(s, place.ahead(d), place.c)

        def store_own(where, value):
            total[s, d, :, where] = value

        share(f, t, store_own)
        to_core(s, d).wait_recv()
        value = total[s, d] + core_in[s, d].astype(jnp.float32)
        if s >= 2:
            b_out[s - 2, d] = value.astype(b_out.dtype)
            to_b(s - 2, d).start()
        else:
            total[s, d] = value

    def cross_a(d):
        to_b(1, d).wait_recv()
        a_out[d] = (total[1, d] + b_in[1, d].astype(jnp.float32)).astype(a_out.dtype)
        to_a(d).start()

    def cross_z(d):
        to_b(0, d).wait_recv()
        to_a(d).wait_recv()
        value = total[0, d] + b_in[0, d].astype(jnp.float32) + a_in[d].astype(jnp.float32)

        @pl.when(d > 0)
        def _():
            z_out[d] = value.astype(z_out.dtype)
            to_z(d).start()

        @pl.when(d == 0)
        def _():
            total[0, d] = value

    def stage(k, carry):
        @pl.when(k < depth)
        def _():
            unit(3, slab(k))
            unit(2, slab(k))

        @pl.when(k > 0)
        def _():
            cross_a(slab(k - 1))

        @pl.when(k < depth)
        def _():
            unit(1, slab(k))
            unit(0, slab(k))

        @pl.when(k > 0)
        def _():
            cross_z(slab(k - 1))

        return carry

    lax.fori_loop(0, depth + 1, stage, 0)
    value = total[0, 0]
    for d in range(1, depth):
        to_z(d).wait_recv()
        value = value + z_in[d].astype(jnp.float32)
    mixed[...] = value.astype(mixed.dtype)

    for d in range(depth):
        if d:
            to_z(d).wait_send()
        to_a(d).wait_send()
        for s in range(2):
            to_b(s, d).wait_send()
        for s in range(4):
            to_core(s, d).wait_send()


def plane_body(
    depth,
    tokens,
    gate_blocks,
    up_blocks,
    down_blocks,
    gate_index,
    up_index,
    down_index,
    gate_count,
    up_count,
    down_count,
):
    rows, feats = tokens.shape
    cols, slots, side = gate_blocks.shape[:3]
    fsdp = 4 * depth
    row_blocks = fsdp * feats // side
    bf16 = tokens.dtype

    first = lax.axis_index("tp") * cols
    index = jnp.stack([gate_index, up_index, down_index])
    count = jnp.stack([gate_count, up_count, down_count])
    index = lax.dynamic_slice_in_dim(index, first, cols, 1)
    count = lax.dynamic_slice_in_dim(count, first, cols, 1)
    slot_ids = jnp.arange(slots, dtype=jnp.int32)[None, None, :, None]
    block_ids = jnp.arange(row_blocks, dtype=jnp.int32)[None, None, None, :]
    hit = (index[..., None] == block_ids) & (slot_ids < count[:, :, None, None])
    slot_of = jnp.min(jnp.where(hit, slot_ids, slots), axis=2)

    vmem = pl.BlockSpec(memory_space=pltpu.VMEM)
    smem = pl.BlockSpec(memory_space=pltpu.SMEM)
    anywhere = pl.BlockSpec(memory_space=pl.ANY)
    dma = pltpu.SemaphoreType.DMA

    hidden = pl.pallas_call(
        functools.partial(in_kernel, depth),
        out_shape=jax.ShapeDtypeStruct((2, rows, cols * side), bf16),
        in_specs=[smem, vmem, anywhere, anywhere],
        out_specs=vmem,
        scratch_shapes=[
            pltpu.VMEM((fsdp, 2, rows, feats), bf16),
            pltpu.VMEM((2, cols, slots + 1, side, side), bf16),
            pltpu.VMEM((2, cols // 2, 2 * rows, 2 * side), jnp.float32),
            dma((2,)),
            dma((2, depth)),
            dma((depth,)),
            dma((2, depth)),
            dma((4, depth)),
            dma((4, depth)),
            dma((4, depth)),
        ],
        compiler_params=pltpu.CompilerParams(
            collective_id=0, has_side_effects=True, vmem_limit_bytes=VMEM_BYTES
        ),
    )(slot_of[:2].reshape(2 * cols, row_blocks), tokens, gate_blocks, up_blocks)

    return pl.pallas_call(
        functools.partial(out_kernel, depth),
        out_shape=jax.ShapeDtypeStruct((rows, feats), bf16),
        in_specs=[smem, vmem, anywhere],
        out_specs=vmem,
        scratch_shapes=[
            pltpu.VMEM((cols, slots + 1, side, side), bf16),
            pltpu.VMEM((4, depth, rows, feats), jnp.float32),
            pltpu.VMEM((4, depth, rows, feats), bf16),
            pltpu.VMEM((4, depth, rows, feats), bf16),
            pltpu.VMEM((2, depth, rows, feats), bf16),
            pltpu.VMEM((2, depth, rows, feats), bf16),
            pltpu.VMEM((depth, rows, feats), bf16),
            pltpu.VMEM((depth, rows, feats), bf16),
            pltpu.VMEM((depth, rows, feats), bf16),
            pltpu.VMEM((depth, rows, feats), bf16),
            dma(()),
            dma((4, depth)),
            dma((4, depth)),
            dma((2, depth)),
            dma((2, depth)),
            dma((depth,)),
            dma((depth,)),
            dma((depth,)),
            dma((depth,)),
        ],
        compiler_params=pltpu.CompilerParams(
            collective_id=1, has_side_effects=True, vmem_limit_bytes=VMEM_BYTES
        ),
    )(slot_of[2], hidden, down_blocks)


def solution(mesh):
    fsdp, tp = mesh.shape["fsdp"], mesh.shape["tp"]
    if tp == 2 and fsdp % 4 == 0:
        body = functools.partial(plane_body, fsdp // 4)
    else:
        body = general_body
    in_specs = (
        P("tp", "fsdp"),
        P(("fsdp", "tp"), None, None, None),
        P(("fsdp", "tp"), None, None, None),
        P(("fsdp", "tp"), None, None, None),
        P("fsdp", None),
        P("fsdp", None),
        P("fsdp", None),
        P("fsdp"),
        P("fsdp"),
        P("fsdp"),
    )
    out_specs = P("tp", "fsdp")
    return jax.shard_map(body, mesh=mesh, in_specs=in_specs, out_specs=out_specs, check_vma=False)
```

```python
import functools

import jax
import jax.numpy as jnp
from jax import lax
from jax.experimental import pallas as pl
from jax.experimental.pallas import tpu as pltpu
from jax.sharding import PartitionSpec as P

MESH = pl.DeviceIdType.MESH
VMEM_BYTES = 62 * 1024 * 1024


def kept_mask(count_part, slot_num):
    return jnp.arange(slot_num, dtype=jnp.int32)[None, :] < count_part[:, None]


def general_body(
    tokens,
    gate_blocks,
    up_blocks,
    down_blocks,
    gate_index,
    up_index,
    down_index,
    gate_count,
    up_count,
    down_count,
):
    whole = lax.all_gather(tokens, "fsdp", axis=1, tiled=True)
    side_len = gate_blocks.shape[-1]
    row_blocks = whole.shape[1] // side_len
    slot_num = gate_index.shape[1]
    block_ids = jnp.arange(row_blocks, dtype=jnp.int32)

    def onehot_of(index_part, count_part):
        live_mask = kept_mask(count_part, slot_num)
        return (
            (index_part[:, :, None] == block_ids[None, None, :]) & live_mask[:, :, None]
        ).astype(jnp.bfloat16)

    def project_in(block_set, index_part, count_part):
        onehot = onehot_of(index_part, count_part)
        panel = jnp.einsum("jki,jkcd->icjd", onehot, block_set, preferred_element_type=jnp.bfloat16)
        panel = panel.reshape(row_blocks * side_len, index_part.shape[0] * side_len)
        return jnp.dot(whole, panel, preferred_element_type=jnp.float32)

    gate_part = project_in(
        lax.all_gather(gate_blocks, "tp", axis=0, tiled=True), gate_index, gate_count
    )
    up_part = project_in(lax.all_gather(up_blocks, "tp", axis=0, tiled=True), up_index, up_count)
    hidden = (jax.nn.silu(gate_part) * up_part).astype(jnp.bfloat16)
    piece = lax.all_gather(down_blocks, "tp", axis=0, tiled=True)
    panel = jnp.einsum(
        "jki,jkcd->jcid",
        onehot_of(down_index, down_count),
        piece,
        preferred_element_type=jnp.bfloat16,
    )
    panel = panel.reshape(piece.shape[0] * side_len, row_blocks * side_len)
    partial_out = jnp.dot(hidden, panel, preferred_element_type=jnp.float32)
    return lax.psum_scatter(partial_out, "fsdp", scatter_dimension=1, tiled=True).astype(
        jnp.bfloat16
    )


class Place:
    def __init__(self, depth):
        fs = lax.axis_index("fsdp")
        self.depth = depth
        self.fs = fs
        self.x = lax.axis_index("tp")
        self.c = fs % 2
        self.y = (fs // 2) % 2
        self.z = fs // 4

    def spot(self, s, z, c):
        across_a, across_b = s % 2, s // 2
        dx = across_b * (1 - c) + across_a * c
        dy = across_a * (1 - c) + across_b * c
        return (z * 2 + (self.y + dy) % 2) * 2 + c, (self.x + dx) % 2

    def order(self, j):
        below, above = self.z, self.depth - 1 - self.z
        near = jnp.minimum(below, above)
        far = j - near
        one_side = jnp.where(below > above, self.z - far, self.z + far)
        both = jnp.where(j % 2 == 1, self.z - (j + 1) // 2, self.z + j // 2)
        return jnp.where(j > 2 * near, one_side, both)

    def ahead(self, d):
        return (self.z + d) % self.depth

    def device(self, s):
        f, t = self.spot(s, self.z, self.c)
        return {"fsdp": f, "tp": t}

    def other_core(self):
        return {"fsdp": self.fs + 1 - 2 * self.c, "tp": self.x}

    def at_z(self, z):
        return {"fsdp": (z * 2 + self.y) * 2 + self.c, "tp": self.x}

    def along_z(self, d):
        return self.at_z(self.ahead(d))


def greet(place):
    barrier = pltpu.get_barrier_semaphore()
    partners = [place.device(1), place.device(2), place.other_core()]
    partners += [place.along_z(d) for d in range(1, place.depth)]
    for partner in partners:
        pl.semaphore_signal(barrier, inc=1, device_id=partner, device_id_type=MESH)
    pl.semaphore_wait(barrier, len(partners))


def remote(src, dst, send_sem, recv_sem, device):
    return pltpu.make_async_remote_copy(
        src_ref=src,
        dst_ref=dst,
        send_sem=send_sem,
        recv_sem=recv_sem,
        device_id=device,
        device_id_type=MESH,
    )


def project_in(
    place,
    depth,
    slot_of,
    loads,
    tokens,
    hidden,
    tok,
    weights,
    acc,
    load_sem,
    z_send,
    a_send,
    b_send,
    c_send,
    plane_recv,
    core_recv,
):
    cols, slots, side = weights.shape[1], weights.shape[2] - 1, weights.shape[3]
    rows, feats = tokens.shape
    blocks = tok.shape[2] // side
    pairs = cols // 2

    def at(f, t):
        row = pl.multiple_of(t * rows, rows)
        col = pl.multiple_of((f % 4) * feats, feats)
        return tok.at[f // 4, pl.ds(row, rows), pl.ds(col, feats)]

    own = pltpu.make_async_copy(tokens, at(place.fs, place.x), load_sem.at[2])
    own.start()
    greet(place)
    own.wait()

    def shard(s, z, c):
        return at(*place.spot(s, z, c))

    def to_a(z):
        ref = shard(0, z, place.c)
        return remote(ref, ref, a_send.at[z], plane_recv.at[1, z], place.device(1))

    def to_b(s, z):
        ref = shard(s, z, place.c)
        return remote(ref, ref, b_send.at[s, z], plane_recv.at[s + 2, z], place.device(2))

    def to_core(s, z):
        ref = shard(s, z, place.c)
        return remote(ref, ref, c_send.at[s, z], core_recv.at[s, z], place.other_core())

    def to_z(up, z):
        ref = shard(0, z, place.c)
        device = place.at_z(place.z + 2 * up - 1)
        return remote(ref, ref, z_send.at[up, z], plane_recv.at[0, z], device)

    def arrived(s, z):
        ref = shard(s, z, place.c)
        remote(ref, ref, c_send.at[s, z], plane_recv.at[s, z], place.other_core()).wait_recv()

    def arrived_core(s, z):
        ref = shard(s, z, 1 - place.c)
        remote(ref, ref, c_send.at[s, z], core_recv.at[s, z], place.other_core()).wait_recv()

    def each_relay(z, act):
        pl.when((z <= place.z) & (place.z < depth - 1))(lambda: act(to_z(1, z)))
        pl.when((z >= place.z) & (place.z > 0))(lambda: act(to_z(0, z)))

    def begin(z):
        each_relay(z, lambda copy: copy.start())
        to_a(z).start()
        to_b(0, z).start()
        to_core(0, z).start()

    def take(j):
        z = place.order(j)
        arrived(0, z)
        begin(z)

    begin(place.z)

    weights[:, :, slots] = jnp.zeros((2, cols, side, side), weights.dtype)
    take(1)
    acc[...] = jnp.zeros_like(acc)
    for load in loads:
        load.wait()

    def multiply(z, n):
        panel = jnp.concatenate(
            [
                jnp.concatenate(
                    [
                        weights[m, 2 * n + e, slot_of[m * cols + 2 * n + e, z * blocks + i]]
                        for m in range(2)
                        for e in range(2)
                    ],
                    axis=1,
                )
                for i in range(blocks)
            ],
            axis=0,
        )
        acc[n] += jnp.dot(tok[z], panel, preferred_element_type=jnp.float32)

    def multiply_some(z, part):
        lax.fori_loop(
            pairs * part // 3, pairs * (part + 1) // 3, lambda n, _: multiply(z, n), None
        )

    def stage(j, carry):
        last = place.order(j - 1)

        @pl.when(j < depth)
        def _():
            z = place.order(j)
            arrived(1, z)
            to_b(1, z).start()
            to_core(1, z).start()

        @pl.when(j + 2 < depth)
        def _():
            take(j + 2)

        @pl.when(j > 0)
        def _():
            for s in range(4):
                arrived_core(s, last)
            multiply_some(last, 0)

        @pl.when(j < depth)
        def _():
            z = place.order(j)
            arrived(2, z)
            to_core(2, z).start()

        @pl.when(j > 0)
        def _():
            multiply_some(last, 1)

        @pl.when(j < depth)
        def _():
            z = place.order(j)
            arrived(3, z)
            to_core(3, z).start()

        @pl.when(j > 0)
        def _():
            multiply_some(last, 2)

        return carry

    lax.fori_loop(0, depth + 1, stage, 0)

    for n in range(pairs):
        gate = acc[n, :, : 2 * side]
        up = acc[n, :, 2 * side :]
        out = (gate / (1.0 + jnp.exp(-gate)) * up).astype(hidden.dtype)
        hidden[:, n * 2 * side : (n + 1) * 2 * side] = out

    for z in range(depth):
        each_relay(z, lambda copy: copy.wait_send())
        to_a(z).wait_send()
        for s in range(2):
            to_b(s, z).wait_send()
        for s in range(4):
            to_core(s, z).wait_send()


def project_out(
    place,
    depth,
    slot_of,
    hidden,
    mixed,
    weights,
    total,
    core_out,
    core_in,
    b_out,
    b_in,
    a_out,
    a_in,
    z_out,
    z_in,
    c_send,
    c_recv,
    b_send,
    b_recv,
    a_send,
    a_recv,
    z_send,
    z_recv,
):
    cols, side = weights.shape[0], weights.shape[2]
    rows = mixed.shape[0]
    group = mixed.shape[1] // side

    def share(d, dy, c, store):
        f = (place.ahead(d) * 2 + (place.y + dy) % 2) * 2 + c
        panel = jnp.concatenate(
            [
                jnp.concatenate(
                    [weights[j, slot_of[j, f * group + i]] for i in range(group)], axis=1
                )
                for j in range(cols)
            ],
            axis=0,
        )
        value = jnp.dot(hidden[...], panel, preferred_element_type=jnp.float32)
        for t in range(2):
            dx = (place.x + t) % 2
            store(dy * (1 + c) + dx * (2 - c), value[t * rows : (t + 1) * rows])

    def to_core(s, d):
        return remote(
            core_out.at[s, d],
            core_in.at[s, d],
            c_send.at[s, d],
            c_recv.at[s, d],
            place.other_core(),
        )

    def to_b(s, d):
        return remote(
            b_out.at[s, d], b_in.at[s, d], b_send.at[s, d], b_recv.at[s, d], place.device(2)
        )

    def to_a(d):
        return remote(a_out.at[d], a_in.at[d], a_send.at[d], a_recv.at[d], place.device(1))

    def to_z(d):
        return remote(z_out.at[d], z_in.at[d], z_send.at[d], z_recv.at[d], place.along_z(d))

    def slab(k):
        return (k + 1) % depth

    def other_share(d, dy):
        def store(s, value):
            core_out[s, d] = value.astype(core_out.dtype)
            to_core(s, d).start()

        share(d, dy, 1 - place.c, store)

    def own_share(d, dy):
        def store(s, value):
            total[s, d] = value

        share(d, dy, place.c, store)

    def unite(s, d):
        to_core(s, d).wait_recv()
        value = total[s, d] + core_in[s, d].astype(jnp.float32)
        if s >= 2:
            b_out[s - 2, d] = value.astype(b_out.dtype)
            to_b(s - 2, d).start()
        else:
            total[s, d] = value

    def cross_a(d):
        to_b(1, d).wait_recv()
        a_out[d] = (total[1, d] + b_in[1, d].astype(jnp.float32)).astype(a_out.dtype)
        to_a(d).start()

    def cross_z(d):
        to_b(0, d).wait_recv()
        to_a(d).wait_recv()
        value = total[0, d] + b_in[0, d].astype(jnp.float32) + a_in[d].astype(jnp.float32)

        @pl.when(d > 0)
        def _():
            z_out[d] = value.astype(z_out.dtype)
            to_z(d).start()

        @pl.when(d == 0)
        def _():
            total[0, d] = value

    def stage(k, carry):
        @pl.when(k < depth)
        def _():
            d = slab(k)
            other_share(d, 1)
            own_share(d, 1)
            unite(3, d)

        @pl.when(k > 1)
        def _():
            cross_z(slab(k - 2))

        @pl.when(k < depth)
        def _():
            d = slab(k)
            other_share(d, 0)
            own_share(d, 0)
            unite(2, d)

        @pl.when((k > 0) & (k < depth + 1))
        def _():
            cross_a(slab(k - 1))

        @pl.when(k < depth)
        def _():
            d = slab(k)
            unite(1, d)
            unite(0, d)

        return carry

    lax.fori_loop(0, depth + 2, stage, 0)
    value = total[0, 0]
    for d in range(1, depth):
        to_z(d).wait_recv()
        value = value + z_in[d].astype(jnp.float32)
    mixed[...] = value.astype(mixed.dtype)

    for d in range(depth):
        if d:
            to_z(d).wait_send()
        to_a(d).wait_send()
        for s in range(2):
            to_b(s, d).wait_send()
        for s in range(4):
            to_core(s, d).wait_send()


def kernel(
    depth,
    in_num,
    in_slots,
    down_slots,
    tokens,
    gate_hbm,
    up_hbm,
    down_hbm,
    mixed,
    hidden,
    in_weights,
    down_weights,
    down_sem,
    *scratch,
):
    place = Place(depth)
    cols, slots, side = down_hbm.shape[0], down_hbm.shape[1], down_hbm.shape[2]
    load_sem = scratch[2]
    loads = [
        pltpu.make_async_copy(src, in_weights.at[m, :, pl.ds(0, slots)], load_sem.at[m])
        for m, src in enumerate((gate_hbm, up_hbm))
    ]
    down_load = pltpu.make_async_copy(down_hbm, down_weights.at[:, pl.ds(0, slots)], down_sem)
    for load in loads:
        load.start()
    down_load.start()
    down_weights[:, slots] = jnp.zeros((cols, side, side), down_weights.dtype)
    tok, acc = scratch[:2]
    project_in(
        place, depth, in_slots, loads, tokens, hidden, tok, in_weights, acc, *scratch[2:in_num]
    )
    down_load.wait()
    project_out(place, depth, down_slots, hidden, mixed, down_weights, *scratch[in_num:])


def plane_body(
    depth,
    tokens,
    gate_blocks,
    up_blocks,
    down_blocks,
    gate_index,
    up_index,
    down_index,
    gate_count,
    up_count,
    down_count,
):
    rows, feats = tokens.shape
    cols, slots, side = gate_blocks.shape[:3]
    fsdp = 4 * depth
    row_blocks = fsdp * feats // side
    bf16 = tokens.dtype

    first = lax.axis_index("tp") * cols
    index = jnp.stack([gate_index, up_index, down_index])
    count = jnp.stack([gate_count, up_count, down_count])
    index = lax.dynamic_slice_in_dim(index, first, cols, 1)
    count = lax.dynamic_slice_in_dim(count, first, cols, 1)
    slot_ids = jnp.arange(slots, dtype=jnp.int32)[None, None, :, None]
    block_ids = jnp.arange(row_blocks, dtype=jnp.int32)[None, None, None, :]
    hit = (index[..., None] == block_ids) & (slot_ids < count[:, :, None, None])
    slot_of = jnp.min(jnp.where(hit, slot_ids, slots), axis=2)

    vmem = pl.BlockSpec(memory_space=pltpu.VMEM)
    smem = pl.BlockSpec(memory_space=pltpu.SMEM)
    anywhere = pl.BlockSpec(memory_space=pl.ANY)
    dma = pltpu.SemaphoreType.DMA

    in_scratch = [
        pltpu.VMEM((depth, 2 * rows, 4 * feats), bf16),
        pltpu.VMEM((cols // 2, 2 * rows, 4 * side), jnp.float32),
        dma((3,)),
        dma((2, depth)),
        dma((depth,)),
        dma((2, depth)),
        dma((4, depth)),
        dma((4, depth)),
        dma((4, depth)),
    ]
    out_scratch = [
        pltpu.VMEM((4, depth, rows, feats), jnp.float32),
        pltpu.VMEM((4, depth, rows, feats), bf16),
        pltpu.VMEM((4, depth, rows, feats), bf16),
        pltpu.VMEM((2, depth, rows, feats), bf16),
        pltpu.VMEM((2, depth, rows, feats), bf16),
        pltpu.VMEM((depth, rows, feats), bf16),
        pltpu.VMEM((depth, rows, feats), bf16),
        pltpu.VMEM((depth, rows, feats), bf16),
        pltpu.VMEM((depth, rows, feats), bf16),
        dma((4, depth)),
        dma((4, depth)),
        dma((2, depth)),
        dma((2, depth)),
        dma((depth,)),
        dma((depth,)),
        dma((depth,)),
        dma((depth,)),
    ]
    return pl.pallas_call(
        functools.partial(kernel, depth, len(in_scratch)),
        out_shape=jax.ShapeDtypeStruct((rows, feats), bf16),
        in_specs=[smem, smem, vmem, anywhere, anywhere, anywhere],
        out_specs=vmem,
        scratch_shapes=[
            pltpu.VMEM((2 * rows, cols * side), bf16),
            pltpu.VMEM((2, cols, slots + 1, side, side), bf16),
            pltpu.VMEM((cols, slots + 1, side, side), bf16),
            dma(()),
        ]
        + in_scratch
        + out_scratch,
        compiler_params=pltpu.CompilerParams(
            collective_id=0, has_side_effects=True, vmem_limit_bytes=VMEM_BYTES
        ),
    )(
        slot_of[:2].reshape(2 * cols, row_blocks),
        slot_of[2],
        tokens,
        gate_blocks,
        up_blocks,
        down_blocks,
    )


def solution(mesh):
    fsdp, tp = mesh.shape["fsdp"], mesh.shape["tp"]
    if tp == 2 and fsdp % 4 == 0 and fsdp >= 8:
        body = functools.partial(plane_body, fsdp // 4)
    else:
        body = general_body
    in_specs = (
        P("tp", "fsdp"),
        P(("fsdp", "tp"), None, None, None),
        P(("fsdp", "tp"), None, None, None),
        P(("fsdp", "tp"), None, None, None),
        P("fsdp", None),
        P("fsdp", None),
        P("fsdp", None),
        P("fsdp"),
        P("fsdp"),
        P("fsdp"),
    )
    out_specs = P("tp", "fsdp")
    return jax.shard_map(body, mesh=mesh, in_specs=in_specs, out_specs=out_specs, check_vma=False)
```

```python
import functools

import jax
import jax.numpy as jnp
from jax import lax
from jax.experimental import pallas as pl
from jax.experimental.pallas import tpu as pltpu
from jax.sharding import PartitionSpec as P

MESH = pl.DeviceIdType.MESH
VMEM_BYTES = 62 * 1024 * 1024


def kept_mask(count_part, slot_num):
    return jnp.arange(slot_num, dtype=jnp.int32)[None, :] < count_part[:, None]


def general_body(
    tokens,
    gate_blocks,
    up_blocks,
    down_blocks,
    gate_index,
    up_index,
    down_index,
    gate_count,
    up_count,
    down_count,
):
    whole = lax.all_gather(tokens, "fsdp", axis=1, tiled=True)
    side_len = gate_blocks.shape[-1]
    row_blocks = whole.shape[1] // side_len
    slot_num = gate_index.shape[1]
    block_ids = jnp.arange(row_blocks, dtype=jnp.int32)

    def onehot_of(index_part, count_part):
        live_mask = kept_mask(count_part, slot_num)
        return (
            (index_part[:, :, None] == block_ids[None, None, :]) & live_mask[:, :, None]
        ).astype(jnp.bfloat16)

    def project_in(block_set, index_part, count_part):
        onehot = onehot_of(index_part, count_part)
        panel = jnp.einsum("jki,jkcd->icjd", onehot, block_set, preferred_element_type=jnp.bfloat16)
        panel = panel.reshape(row_blocks * side_len, index_part.shape[0] * side_len)
        return jnp.dot(whole, panel, preferred_element_type=jnp.float32)

    gate_part = project_in(
        lax.all_gather(gate_blocks, "tp", axis=0, tiled=True), gate_index, gate_count
    )
    up_part = project_in(lax.all_gather(up_blocks, "tp", axis=0, tiled=True), up_index, up_count)
    hidden = (jax.nn.silu(gate_part) * up_part).astype(jnp.bfloat16)
    piece = lax.all_gather(down_blocks, "tp", axis=0, tiled=True)
    panel = jnp.einsum(
        "jki,jkcd->jcid",
        onehot_of(down_index, down_count),
        piece,
        preferred_element_type=jnp.bfloat16,
    )
    panel = panel.reshape(piece.shape[0] * side_len, row_blocks * side_len)
    partial_out = jnp.dot(hidden, panel, preferred_element_type=jnp.float32)
    return lax.psum_scatter(partial_out, "fsdp", scatter_dimension=1, tiled=True).astype(
        jnp.bfloat16
    )


class Place:
    def __init__(self, depth):
        fs = lax.axis_index("fsdp")
        self.depth = depth
        self.fs = fs
        self.x = lax.axis_index("tp")
        self.c = fs % 2
        self.y = (fs // 2) % 2
        self.z = fs // 4

    def spot(self, s, z, c):
        across_a, across_b = s % 2, s // 2
        dx = across_b * (1 - c) + across_a * c
        dy = across_a * (1 - c) + across_b * c
        return (z * 2 + (self.y + dy) % 2) * 2 + c, (self.x + dx) % 2

    def order(self, j):
        below, above = self.z, self.depth - 1 - self.z
        near = jnp.minimum(below, above)
        far = j - near
        one_side = jnp.where(below > above, self.z - far, self.z + far)
        both = jnp.where(j % 2 == 1, self.z - (j + 1) // 2, self.z + j // 2)
        return jnp.where(j > 2 * near, one_side, both)

    def ahead(self, d):
        return (self.z + d) % self.depth

    def device(self, s):
        f, t = self.spot(s, self.z, self.c)
        return {"fsdp": f, "tp": t}

    def other_core(self):
        return {"fsdp": self.fs + 1 - 2 * self.c, "tp": self.x}

    def at_z(self, z):
        return {"fsdp": (z * 2 + self.y) * 2 + self.c, "tp": self.x}

    def along_z(self, d):
        return self.at_z(self.ahead(d))


def greet(place):
    barrier = pltpu.get_barrier_semaphore()
    partners = [place.device(1), place.device(2), place.other_core()]
    partners += [place.along_z(d) for d in range(1, place.depth)]
    for partner in partners:
        pl.semaphore_signal(barrier, inc=1, device_id=partner, device_id_type=MESH)
    pl.semaphore_wait(barrier, len(partners))


def remote(src, dst, send_sem, recv_sem, device):
    return pltpu.make_async_remote_copy(
        src_ref=src,
        dst_ref=dst,
        send_sem=send_sem,
        recv_sem=recv_sem,
        device_id=device,
        device_id_type=MESH,
    )


def project_in(
    place,
    depth,
    slot_of,
    loads,
    tokens,
    hidden,
    tok,
    weights,
    acc,
    load_sem,
    z_send,
    a_send,
    b_send,
    c_send,
    plane_recv,
    core_recv,
):
    cols, slots, side = weights.shape[1], weights.shape[2] - 1, weights.shape[3]
    rows, feats = tokens.shape
    blocks = tok.shape[2] // side
    pairs = cols // 2

    def at(f, t):
        row = pl.multiple_of(t * rows, rows)
        col = pl.multiple_of((f % 4) * feats, feats)
        return tok.at[f // 4, pl.ds(row, rows), pl.ds(col, feats)]

    own = pltpu.make_async_copy(tokens, at(place.fs, place.x), load_sem.at[2])
    own.start()
    greet(place)
    own.wait()

    def shard(s, z, c):
        return at(*place.spot(s, z, c))

    def to_a(z):
        ref = shard(0, z, place.c)
        return remote(ref, ref, a_send.at[z], plane_recv.at[1, z], place.device(1))

    def to_b(s, z):
        ref = shard(s, z, place.c)
        return remote(ref, ref, b_send.at[s, z], plane_recv.at[s + 2, z], place.device(2))

    def to_core(s, z):
        ref = shard(s, z, place.c)
        return remote(ref, ref, c_send.at[s, z], core_recv.at[s, z], place.other_core())

    def to_z(up, z):
        ref = shard(0, z, place.c)
        device = place.at_z(place.z + 2 * up - 1)
        return remote(ref, ref, z_send.at[up, z], plane_recv.at[0, z], device)

    def arrived(s, z):
        ref = shard(s, z, place.c)
        remote(ref, ref, c_send.at[s, z], plane_recv.at[s, z], place.other_core()).wait_recv()

    def arrived_core(s, z):
        ref = shard(s, z, 1 - place.c)
        remote(ref, ref, c_send.at[s, z], core_recv.at[s, z], place.other_core()).wait_recv()

    def each_relay(z, act):
        pl.when((z <= place.z) & (place.z < depth - 1))(lambda: act(to_z(1, z)))
        pl.when((z >= place.z) & (place.z > 0))(lambda: act(to_z(0, z)))

    def begin(z):
        each_relay(z, lambda copy: copy.start())
        to_a(z).start()
        to_b(0, z).start()
        to_core(0, z).start()

    def take(j):
        z = place.order(j)
        arrived(0, z)
        begin(z)

    begin(place.z)

    weights[:, :, slots] = jnp.zeros((2, cols, side, side), weights.dtype)
    take(1)
    acc[...] = jnp.zeros_like(acc)
    for load in loads:
        load.wait()

    def multiply(z, n):
        panel = jnp.concatenate(
            [
                jnp.concatenate(
                    [
                        weights[m, 2 * n + e, slot_of[m * cols + 2 * n + e, z * blocks + i]]
                        for m in range(2)
                        for e in range(2)
                    ],
                    axis=1,
                )
                for i in range(blocks)
            ],
            axis=0,
        )
        acc[n] += jnp.dot(tok[z], panel, preferred_element_type=jnp.float32)

    def multiply_some(z, part):
        lax.fori_loop(
            pairs * part // 3, pairs * (part + 1) // 3, lambda n, _: multiply(z, n), None
        )

    def stage(j, carry):
        last = place.order(j - 1)

        @pl.when(j < depth)
        def _():
            z = place.order(j)
            arrived(1, z)
            to_b(1, z).start()
            to_core(1, z).start()

        @pl.when(j + 2 < depth)
        def _():
            take(j + 2)

        @pl.when(j > 0)
        def _():
            for s in range(4):
                arrived_core(s, last)
            multiply_some(last, 0)

        @pl.when(j < depth)
        def _():
            z = place.order(j)
            arrived(2, z)
            to_core(2, z).start()

        @pl.when(j > 0)
        def _():
            multiply_some(last, 1)

        @pl.when(j < depth)
        def _():
            z = place.order(j)
            arrived(3, z)
            to_core(3, z).start()

        @pl.when(j > 0)
        def _():
            multiply_some(last, 2)

        return carry

    lax.fori_loop(0, depth + 1, stage, 0)

    for n in range(pairs):
        gate = acc[n, :, : 2 * side]
        up = acc[n, :, 2 * side :]
        out = (gate / (1.0 + jnp.exp(-gate)) * up).astype(hidden.dtype)
        hidden[:, n * 2 * side : (n + 1) * 2 * side] = out

    for z in range(depth):
        each_relay(z, lambda copy: copy.wait_send())
        to_a(z).wait_send()
        for s in range(2):
            to_b(s, z).wait_send()
        for s in range(4):
            to_core(s, z).wait_send()


def project_out(
    place,
    depth,
    slot_of,
    hidden,
    mixed,
    weights,
    total,
    core_out,
    core_in,
    b_out,
    b_in,
    a_out,
    a_in,
    z_out,
    z_in,
    c_send,
    c_recv,
    b_send,
    b_recv,
    a_send,
    a_recv,
    z_send,
    z_recv,
):
    cols, side = weights.shape[0], weights.shape[2]
    rows = mixed.shape[0]
    group = mixed.shape[1] // side

    def share(d, dy, c, store):
        f = (place.ahead(d) * 2 + (place.y + dy) % 2) * 2 + c
        panel = jnp.concatenate(
            [
                jnp.concatenate(
                    [weights[j, slot_of[2 * cols + j, f * group + i]] for i in range(group)], axis=1
                )
                for j in range(cols)
            ],
            axis=0,
        )
        value = jnp.dot(hidden[...], panel, preferred_element_type=jnp.float32)
        for t in range(2):
            dx = (place.x + t) % 2
            store(dy * (1 + c) + dx * (2 - c), value[t * rows : (t + 1) * rows])

    def to_core(s, d):
        return remote(
            core_out.at[s, d],
            core_in.at[s, d],
            c_send.at[s, d],
            c_recv.at[s, d],
            place.other_core(),
        )

    def to_b(s, d):
        return remote(
            b_out.at[s, d], b_in.at[s, d], b_send.at[s, d], b_recv.at[s, d], place.device(2)
        )

    def to_a(d):
        return remote(a_out.at[d], a_in.at[d], a_send.at[d], a_recv.at[d], place.device(1))

    def to_z(d):
        return remote(z_out.at[d], z_in.at[d], z_send.at[d], z_recv.at[d], place.along_z(d))

    def slab(k):
        return (k + 1) % depth

    def other_share(d, dy):
        def store(s, value):
            core_out[s, d] = value.astype(core_out.dtype)
            to_core(s, d).start()

        share(d, dy, 1 - place.c, store)

    def own_share(d, dy):
        def store(s, value):
            total[s, d] = value

        share(d, dy, place.c, store)

    def unite(s, d):
        to_core(s, d).wait_recv()
        value = total[s, d] + core_in[s, d].astype(jnp.float32)
        if s >= 2:
            b_out[s - 2, d] = value.astype(b_out.dtype)
            to_b(s - 2, d).start()
        else:
            total[s, d] = value

    def cross_a(d):
        to_b(1, d).wait_recv()
        a_out[d] = (total[1, d] + b_in[1, d].astype(jnp.float32)).astype(a_out.dtype)
        to_a(d).start()

    def cross_z(d):
        to_b(0, d).wait_recv()
        to_a(d).wait_recv()
        value = total[0, d] + b_in[0, d].astype(jnp.float32) + a_in[d].astype(jnp.float32)

        @pl.when(d > 0)
        def _():
            z_out[d] = value.astype(z_out.dtype)
            to_z(d).start()

        @pl.when(d == 0)
        def _():
            total[0, d] = value

    def stage(k, carry):
        @pl.when(k < depth)
        def _():
            d = slab(k)
            other_share(d, 1)
            own_share(d, 1)
            unite(3, d)
            pl.when(place.c == 1)(lambda: unite(2, d))

        @pl.when(k > 1)
        def _():
            cross_z(slab(k - 2))

        @pl.when(k < depth)
        def _():
            d = slab(k)
            other_share(d, 0)
            own_share(d, 0)
            pl.when(place.c == 0)(lambda: unite(2, d))

        @pl.when((k > 0) & (k < depth + 1))
        def _():
            cross_a(slab(k - 1))

        @pl.when(k < depth)
        def _():
            d = slab(k)
            unite(1, d)
            unite(0, d)

        return carry

    lax.fori_loop(0, depth + 2, stage, 0)
    value = total[0, 0]
    for d in range(1, depth):
        to_z(d).wait_recv()
        value = value + z_in[d].astype(jnp.float32)
    mixed[...] = value.astype(mixed.dtype)

    for d in range(depth):
        if d:
            to_z(d).wait_send()
        to_a(d).wait_send()
        for s in range(2):
            to_b(s, d).wait_send()
        for s in range(4):
            to_core(s, d).wait_send()


def kernel(
    depth,
    in_num,
    slot_of,
    tokens,
    gate_hbm,
    up_hbm,
    down_hbm,
    mixed,
    hidden,
    in_weights,
    down_weights,
    down_sem,
    *scratch,
):
    place = Place(depth)
    cols, slots, side = down_hbm.shape[0], down_hbm.shape[1], down_hbm.shape[2]
    load_sem = scratch[2]
    loads = [
        pltpu.make_async_copy(src, in_weights.at[m, :, pl.ds(0, slots)], load_sem.at[m])
        for m, src in enumerate((gate_hbm, up_hbm))
    ]
    down_load = pltpu.make_async_copy(down_hbm, down_weights.at[:, pl.ds(0, slots)], down_sem)
    for load in loads:
        load.start()
    down_load.start()
    down_weights[:, slots] = jnp.zeros((cols, side, side), down_weights.dtype)
    tok, acc = scratch[:2]
    project_in(
        place, depth, slot_of, loads, tokens, hidden, tok, in_weights, acc, *scratch[2:in_num]
    )
    down_load.wait()
    project_out(place, depth, slot_of, hidden, mixed, down_weights, *scratch[in_num:])


def plane_body(
    depth,
    tokens,
    gate_blocks,
    up_blocks,
    down_blocks,
    gate_index,
    up_index,
    down_index,
    gate_count,
    up_count,
    down_count,
):
    rows, feats = tokens.shape
    cols, slots, side = gate_blocks.shape[:3]
    fsdp = 4 * depth
    row_blocks = fsdp * feats // side
    bf16 = tokens.dtype

    first = lax.axis_index("tp") * cols
    index = jnp.stack([gate_index, up_index, down_index])
    count = jnp.stack([gate_count, up_count, down_count])
    index = lax.dynamic_slice_in_dim(index, first, cols, 1)
    count = lax.dynamic_slice_in_dim(count, first, cols, 1)
    slot_ids = jnp.arange(slots, dtype=jnp.int32)[None, None, :, None]
    block_ids = jnp.arange(row_blocks, dtype=jnp.int32)[None, None, None, :]
    hit = (index[..., None] == block_ids) & (slot_ids < count[:, :, None, None])
    slot_of = jnp.min(jnp.where(hit, slot_ids, slots), axis=2)

    vmem = pl.BlockSpec(memory_space=pltpu.VMEM)
    smem = pl.BlockSpec(memory_space=pltpu.SMEM)
    anywhere = pl.BlockSpec(memory_space=pl.ANY)
    dma = pltpu.SemaphoreType.DMA

    in_scratch = [
        pltpu.VMEM((depth, 2 * rows, 4 * feats), bf16),
        pltpu.VMEM((cols // 2, 2 * rows, 4 * side), jnp.float32),
        dma((3,)),
        dma((2, depth)),
        dma((depth,)),
        dma((2, depth)),
        dma((4, depth)),
        dma((4, depth)),
        dma((4, depth)),
    ]
    out_scratch = [
        pltpu.VMEM((4, depth, rows, feats), jnp.float32),
        pltpu.VMEM((4, depth, rows, feats), bf16),
        pltpu.VMEM((4, depth, rows, feats), bf16),
        pltpu.VMEM((2, depth, rows, feats), bf16),
        pltpu.VMEM((2, depth, rows, feats), bf16),
        pltpu.VMEM((depth, rows, feats), bf16),
        pltpu.VMEM((depth, rows, feats), bf16),
        pltpu.VMEM((depth, rows, feats), bf16),
        pltpu.VMEM((depth, rows, feats), bf16),
        dma((4, depth)),
        dma((4, depth)),
        dma((2, depth)),
        dma((2, depth)),
        dma((depth,)),
        dma((depth,)),
        dma((depth,)),
        dma((depth,)),
    ]
    return pl.pallas_call(
        functools.partial(kernel, depth, len(in_scratch)),
        out_shape=jax.ShapeDtypeStruct((rows, feats), bf16),
        in_specs=[smem, vmem, anywhere, anywhere, anywhere],
        out_specs=vmem,
        scratch_shapes=[
            pltpu.VMEM((2 * rows, cols * side), bf16),
            pltpu.VMEM((2, cols, slots + 1, side, side), bf16),
            pltpu.VMEM((cols, slots + 1, side, side), bf16),
            dma(()),
        ]
        + in_scratch
        + out_scratch,
        compiler_params=pltpu.CompilerParams(
            collective_id=0, has_side_effects=True, vmem_limit_bytes=VMEM_BYTES
        ),
    )(
        slot_of.reshape(3 * cols, row_blocks),
        tokens,
        gate_blocks,
        up_blocks,
        down_blocks,
    )


def solution(mesh):
    fsdp, tp = mesh.shape["fsdp"], mesh.shape["tp"]
    if tp == 2 and fsdp % 4 == 0 and fsdp >= 8:
        body = functools.partial(plane_body, fsdp // 4)
    else:
        body = general_body
    in_specs = (
        P("tp", "fsdp"),
        P(("fsdp", "tp"), None, None, None),
        P(("fsdp", "tp"), None, None, None),
        P(("fsdp", "tp"), None, None, None),
        P("fsdp", None),
        P("fsdp", None),
        P("fsdp", None),
        P("fsdp"),
        P("fsdp"),
        P("fsdp"),
    )
    out_specs = P("tp", "fsdp")
    return jax.shard_map(body, mesh=mesh, in_specs=in_specs, out_specs=out_specs, check_vma=False)
```
